32 devices in a mesh: rep: 2 (over x), tp: 16 (over z, y, core).
Axes of the slice: x: 2, y: 2, z: 4, core: 2. Of those that a mesh axis runs over, the one named last changes fastest.
Arguments:
- hidden_codes: bfloat16 [256, 34816], P('rep', 'tp'), parts along dimension 0, may hold values from -127 to 127, as said below
- hidden_scale: float32 [256], P('rep'), parts along dimension 0, may hold values from 0.0005 to 0.005
- down_codes: bfloat16 [34816, 16384], P('tp'), may hold values from -127 to 127, as said below
- weight_scale: float32 [16384], replicated, may hold values from 0.0006 to 0.006
- residual: bfloat16 [256, 16384], P('rep', 'tp'), parts along dimension 0, may hold values from -6 to 6
Outputs:
- mixed: bfloat16 [256, 16384], P('rep'), parts along dimension 0
The draws below stay inside these ranges and needn't reach their ends.
There are 2 independent parts, one for each index of `rep`. The reference program is written for one: setup_inputs(seed, part) draws one part's arguments, and reference() takes and returns one part's arrays. A program takes and returns all parts, laid end to end along the dimension named above; an argument that names none is the same for every part. Nothing has to cross between parts.
Inputs may be any that keep to these rules, and one draw needn't show every extreme that they name: `hidden_codes`: whole numbers; every token's row holds a code of magnitude 127. `down_codes`: whole numbers; every output channel's column holds a code of magnitude 127.
All inputs are finite; a program needn't handle non-finite values. Where the reference program divides by a largest or mean magnitude, that divisor is 1e-20 or more.
Results may differ from the reference program's by a relative error of at most 0.012.
Values may be sent and summed in bfloat16 or wider, within the bound.
A program may use at most 320 MiB of HBM per device.

```python
import math
import jax
import jax.numpy as jnp
from jax import lax

D = 16384
FF = 34816
BLOCK = 128
TOKENS = 128
FF_SLICE = 2176
N_TP = 16


def draw_hidden_codes(key, part):
    key = jax.random.fold_in(key, 11)
    first_key, second_key = jax.random.split(key)
    codes = jax.random.randint(first_key, (TOKENS, FF), -127, 128)
    column = jax.random.randint(second_key, (TOKENS, 1), 0, FF)
    parity = 1 - 2 * (jnp.arange(TOKENS)[:, None] % 2)
    codes = jnp.where(jnp.arange(FF)[None, :] == column, 127 * parity, codes)
    return codes.astype(jnp.float32).astype(jnp.bfloat16)


def draw_down_codes(key, part):
    key = jax.random.fold_in(key, 23)
    strong_key, weak_key, order_key, row_key = jax.random.split(key, 4)
    pairing = jax.random.permutation(order_key, N_TP)
    owner = jnp.arange(FF) // FF_SLICE
    channel_block = jnp.arange(D) // (D // N_TP)
    strong = pairing[owner][:, None] == channel_block[None, :]
    strong_codes = jax.random.randint(strong_key, (FF, D), -127, 128)
    weak_codes = jax.random.randint(weak_key, (FF, D), -42, 43)
    codes = jnp.where(strong, strong_codes, weak_codes)
    row = jax.random.randint(row_key, (1, D), 0, FF)
    parity = 1 - 2 * (jnp.arange(D)[None, :] % 2)
    codes = jnp.where(jnp.arange(FF)[:, None] == row, 127 * parity, codes)
    return codes.astype(jnp.float32).astype(jnp.bfloat16)


def steps_of(stream_key, shape, cuts, least, high):
    def one(dim, blocks):
        steps = jax.random.uniform(jax.random.fold_in(jax.random.fold_in(stream_key, 6), dim), (blocks,), jnp.float32, least / len(cuts), high / len(cuts))
        return jnp.repeat(jnp.exp(steps), shape[dim] // blocks).reshape((-1,) + (1,) * (len(shape) - dim - 1))

    factor_of = one(*cuts[0])
    for cut in cuts[1:]:
        factor_of = factor_of * one(*cut)
    return factor_of


def noise(stream_key, dims, deviation, bound, cuts=(), kind=jnp.bfloat16):
    entries = jax.random.normal(stream_key, dims, jnp.float32) * deviation
    if len(cuts) > 0:
        entries = steps_of(stream_key, dims, cuts, -0.22, 0.18) * entries
    return jnp.clip(entries, min=-bound, max=bound).astype(kind)


def setup_inputs(seed: int = 0, part: int = 0) -> dict:
    key_list = jax.random.split(jax.random.key(seed), 6)
    part_splits = jax.random.split(jax.random.fold_in(key_list[5], part), 6)
    return {
        "hidden_codes": draw_hidden_codes(jax.random.fold_in(jax.random.fold_in(key_list[5], part), 71), part),
        "hidden_scale": jnp.clip(jnp.exp(jax.random.uniform(part_splits[1], (TOKENS,), jnp.float32, math.log(0.0005), math.log(0.005))), 0.0005, 0.005),
        "down_codes": draw_down_codes(jax.random.fold_in(key_list[5], 71), part),
        "weight_scale": jnp.clip(jnp.exp(jax.random.uniform(key_list[3], (D,), jnp.float32, math.log(0.0006), math.log(0.006))), 0.0006, 0.006),
        "residual": noise(part_splits[4], (TOKENS, D), 1.0, 6.0, ((1, 16),)),
    }


def code_blocks(values):
    grouped = values.reshape(values.shape[0], -1, BLOCK)
    block_scale = jnp.max(jnp.abs(grouped), axis=2) + 1e-6
    coded = (grouped / block_scale[:, :, None]).astype(jnp.bfloat16)
    return coded, block_scale


def reference(hidden_codes, hidden_scale, down_codes, weight_scale, residual):
    def add_slice(slice_index, running):
        first_unit = (jnp.asarray(slice_index).astype(jnp.int32) * FF_SLICE).astype(jnp.int32)
        left_rows = lax.dynamic_slice_in_dim(hidden_codes, first_unit, FF_SLICE, 1)
        right_rows = lax.dynamic_slice_in_dim(down_codes, first_unit, FF_SLICE, 0)
        partial_value = jnp.dot(left_rows, right_rows, preferred_element_type=jnp.float32)
        partial_value = partial_value * hidden_scale[:, None] * weight_scale[None, :]
        coded, block_scale = code_blocks(partial_value)
        decoded = coded.astype(jnp.float32) * block_scale[:, :, None]
        return running + decoded.reshape(running.shape)

    summed = lax.fori_loop(0, N_TP, add_slice, jnp.zeros((TOKENS, D), jnp.float32))
    total = residual.astype(jnp.float32) + summed
    coded, block_scale = code_blocks(total)
    return (coded.astype(jnp.float32) * block_scale[:, :, None]).reshape(TOKENS, D).astype(jnp.bfloat16)
```

```python
import functools

import jax
import jax.numpy as jnp
from jax import lax
from jax.experimental import pallas as pl
from jax.experimental.pallas import tpu as pltpu
from jax.sharding import PartitionSpec as P

BLOCK = 128
CORES = 2
WIDTH = 256
BUFFERS = 8
MESH = pl.DeviceIdType.MESH


def grid_of(devices):
    chips = devices // CORES
    inner = 1
    while (2 * inner) ** 2 <= chips:
        inner *= 2
    return chips // inner, inner


def kernel(
    nz, ny, width, chunks,
    hid_ref, hs_ref, ws_ref, res_ref, w_ref, out_ref,
    wbuf, mine, cs, cr, ys, yr, zs, zr, fin,
    wsem, cs_sem, cr_sem, ys_sem, yr_sem, zs_sem, zr_sem, loc_sem,
    gzs_sem, gzr_sem, gys_sem, gyr_sem, gcs_sem, gcr_sem,
):
    me = lax.axis_index("tp")
    c = lax.rem(me, CORES)
    y = lax.rem(me // CORES, ny)
    z = me // (CORES * ny)
    owned = chunks * width
    tiles = ny * nz
    total_tiles = chunks * 2 * tiles

    def device(zi, yi, ci):
        return {"tp": (zi * ny + yi) * CORES + ci}

    partner = device(z, y, 1 - c)
    y_of = [lax.rem(y + j, ny) for j in range(ny)]
    z_of = [lax.rem(z + j, nz) for j in range(nz)]

    def column(t):
        k = t // (2 * tiles)
        h = lax.rem(t // tiles, 2)
        i = lax.rem(t, tiles)
        core = jnp.where(h == 0, 1 - c, c)
        owner = (lax.rem(i, nz) * ny + i // nz) * CORES + core
        return pl.multiple_of(owner * owned + k * width, 128)

    def fetch(t):
        slot = lax.rem(t, BUFFERS)
        return pltpu.make_async_copy(
            w_ref.at[:, pl.ds(column(t), width)], wbuf.at[slot], wsem.at[slot]
        )

    for t in range(min(BUFFERS - 1, total_tiles)):
        fetch(jnp.int32(t)).start()

    barrier = pltpu.get_barrier_semaphore()
    peers = [partner]
    peers += [device(z, y_of[j], c) for j in range(1, ny)]
    peers += [device(z_of[j], y, c) for j in range(1, nz)]
    for peer in peers:
        pl.semaphore_signal(barrier, inc=1, device_id=peer, device_id_type=MESH)
    pl.semaphore_wait(barrier, len(peers))

    def remote(src, dst, send, recv, peer):
        return pltpu.make_async_remote_copy(
            src_ref=src, dst_ref=dst, send_sem=send, recv_sem=recv,
            device_id=peer, device_id_type=MESH,
        )

    def core_copy(k):
        return remote(cs.at[k], cr.at[k], cs_sem.at[k], cr_sem.at[k], partner)

    def y_copy(k, j):
        return remote(ys.at[k, j - 1], yr.at[k, j - 1], ys_sem.at[k, j - 1],
                      yr_sem.at[k, j - 1], device(z, y_of[j], c))

    def z_copy(k, j):
        return remote(zs.at[k, j - 1], zr.at[k, j - 1], zs_sem.at[k, j - 1],
                      zr_sem.at[k, j - 1], device(z_of[j], y, c))

    def local_copy(k):
        return pltpu.make_async_copy(fin.at[k], out_ref.at[k, c, y, z], loc_sem.at[k])

    def gather_z(k, j):
        block = out_ref.at[k, c, y, z]
        return remote(fin.at[k], block, gzs_sem.at[k, j - 1], gzr_sem.at[k, j - 1],
                      device(z_of[j], y, c))

    def gather_y(k, j):
        block = out_ref.at[k, c, y]
        return remote(block, block, gys_sem.at[k, j - 1], gyr_sem.at[k, j - 1],
                      device(z, y_of[j], c))

    def gather_core(k):
        block = out_ref.at[k, c]
        return remote(block, block, gcs_sem.at[k], gcr_sem.at[k], partner)

    def multiply(k, h):
        first = (k * 2 + h) * tiles

        @pl.loop(0, tiles)
        def _(i):
            t = first + i

            @pl.when(t + BUFFERS - 1 < total_tiles)
            def _():
                fetch(t + BUFFERS - 1).start()

            fetch(t).wait()
            value = jnp.dot(
                hid_ref[...], wbuf[lax.rem(t, BUFFERS)], preferred_element_type=jnp.float32
            )
            value = value * hs_ref[...] * ws_ref[:, pl.ds(column(t), width)]
            if h == 0:
                cs[k, i // nz, lax.rem(i, nz)] = value.astype(cs.dtype)
            else:
                mine[k, i // nz, lax.rem(i, nz)] = value

    def send_y(k):
        core_copy(k).wait_recv()
        for j in range(1, ny):
            @pl.loop(0, nz)
            def _(b):
                ys[k, j - 1, b] = (
                    mine[k, y_of[j], b] + cr[k, y_of[j], b].astype(jnp.float32)
                ).astype(ys.dtype)

            y_copy(k, j).start()

        @pl.loop(0, nz)
        def _(b):
            mine[k, y, b] += cr[k, y, b].astype(jnp.float32)

    def send_z(k):
        for j in range(1, ny):
            y_copy(k, j).wait_recv()

        def total(b):
            value = mine[k, y, b]
            for j in range(1, ny):
                value += yr[k, j - 1, b].astype(jnp.float32)
            return value

        for j in range(1, nz):
            zs[k, j - 1] = total(z_of[j]).astype(zs.dtype)
            z_copy(k, j).start()
        mine[k, y, z] = total(z)

    def finish(k):
        value = mine[k, y, z] + res_ref[:, k * width:(k + 1) * width].astype(jnp.float32)
        for j in range(1, nz):
            z_copy(k, j).wait_recv()
            value += zr[k, j - 1].astype(jnp.float32)
        for b in range(width // BLOCK):
            part = value[:, b * BLOCK:(b + 1) * BLOCK]
            scale = jnp.max(jnp.abs(part), axis=1, keepdims=True) + 1e-6
            code = (part / scale).astype(jnp.bfloat16)
            fin[k, :, b * BLOCK:(b + 1) * BLOCK] = (
                code.astype(jnp.float32) * scale
            ).astype(fin.dtype)
        for j in range(1, nz):
            gather_z(k, j).start()
        local_copy(k).start()

    def pass_y(k):
        local_copy(k).wait()
        for j in range(1, nz):
            gather_z(k, j).wait_recv()
        for j in range(1, ny):
            gather_y(k, j).start()

    def pass_core(k):
        for j in range(1, ny):
            gather_y(k, j).wait_recv()
        gather_core(k).start()

    def drain(k):
        gather_core(k).wait()
        core_copy(k).wait_send()
        for j in range(1, ny):
            y_copy(k, j).wait_send()
            gather_y(k, j).wait_send()
        for j in range(1, nz):
            z_copy(k, j).wait_send()
            gather_z(k, j).wait_send()

    stages = ((send_y, 1), (send_z, 3), (finish, 5), (pass_y, 7), (pass_core, 9))
    for u in range(2 * chunks + 8):
        k, h = u // 2, u % 2
        if k < chunks:
            multiply(k, h)
            if h == 0:
                core_copy(k).start()
        for stage, lag in reversed(stages):
            if (u - lag) % 2 == 0 and 0 <= (u - lag) // 2 < chunks:
                stage((u - lag) // 2)
    for k in range(chunks):
        drain(k)


def shards(hidden_codes, hidden_scale, down_codes, weight_scale, residual):
    devices = lax.axis_size("tp")
    nz, ny = grid_of(devices)
    rows, depth = hidden_codes.shape
    model_width = down_codes.shape[1]
    owned = model_width // devices
    width = min(WIDTH, owned)
    chunks = owned // width
    bf16, f32 = jnp.bfloat16, jnp.float32
    vmem = pl.BlockSpec(memory_space=pltpu.VMEM)
    dma = pltpu.SemaphoreType.DMA
    tile = (rows, width)
    got = pl.pallas_call(
        functools.partial(kernel, nz, ny, width, chunks),
        out_shape=jax.ShapeDtypeStruct((chunks, CORES, ny, nz) + tile, bf16),
        in_specs=[vmem, vmem, vmem, vmem, pl.BlockSpec(memory_space=pl.ANY)],
        out_specs=pl.BlockSpec(memory_space=pl.ANY),
        scratch_shapes=[
            pltpu.VMEM((BUFFERS, depth, width), bf16),
            pltpu.VMEM((chunks, ny, nz) + tile, f32),
            pltpu.VMEM((chunks, ny, nz) + tile, bf16),
            pltpu.VMEM((chunks, ny, nz) + tile, bf16),
            pltpu.VMEM((chunks, ny - 1, nz) + tile, bf16),
            pltpu.VMEM((chunks, ny - 1, nz) + tile, bf16),
            pltpu.VMEM((chunks, nz - 1) + tile, bf16),
            pltpu.VMEM((chunks, nz - 1) + tile, bf16),
            pltpu.VMEM((chunks,) + tile, bf16),
            dma((BUFFERS,)), dma((chunks,)), dma((chunks,)),
            dma((chunks, ny - 1)), dma((chunks, ny - 1)),
            dma((chunks, nz - 1)), dma((chunks, nz - 1)), dma((chunks,)),
            dma((chunks, nz - 1)), dma((chunks, nz - 1)),
            dma((chunks, ny - 1)), dma((chunks, ny - 1)),
            dma((chunks,)), dma((chunks,)),
        ],
        compiler_params=pltpu.CompilerParams(
            collective_id=0, has_side_effects=True, vmem_limit_bytes=48 * 1024 * 1024
        ),
        cost_estimate=pl.CostEstimate(
            flops=2 * rows * depth * model_width,
            bytes_accessed=2 * depth * model_width,
            transcendentals=0,
        ),
    )(hidden_codes, hidden_scale[:, None], weight_scale[None, :], residual, down_codes)
    got = jnp.transpose(got, (4, 3, 2, 1, 0, 5))
    return got.reshape(rows, model_width)


def solution(mesh):
    placed = (P("rep", "tp"), P("rep"), P("tp", None), P(), P("rep", "tp"))
    return jax.shard_map(
        shards, mesh=mesh, in_specs=placed, out_specs=P("rep", None), check_vma=False
    )
```

```python
import functools

import jax
import jax.numpy as jnp
from jax import lax
from jax.experimental import pallas as pl
from jax.experimental.pallas import tpu as pltpu
from jax.sharding import PartitionSpec as P

BLOCK = 128
CORES = 2
WIDTH = 256
BUFFERS = 8
MESH = pl.DeviceIdType.MESH


def grid_of(devices):
    chips = devices // CORES
    inner = 1
    while (2 * inner) ** 2 <= chips:
        inner *= 2
    return chips // inner, inner


def kernel(
    nz, ny, width, chunks,
    hid_ref, hs_ref, ws_ref, res_ref, w_ref, out_ref,
    wbuf, mine, cs, cr, ys, yr, zs, zr, fin,
    wsem, cs_sem, cr_sem, ys_sem, yr_sem, zs_sem, zr_sem, loc_sem,
    gzs_sem, gzr_sem, gys_sem, gyr_sem, gcs_sem, gcr_sem,
):
    me = lax.axis_index("tp")
    c = lax.rem(me, CORES)
    y = lax.rem(me // CORES, ny)
    z = me // (CORES * ny)
    owned = chunks * width
    tiles = ny * nz
    total_tiles = chunks * 2 * tiles

    def device(zi, yi, ci):
        return {"tp": (zi * ny + yi) * CORES + ci}

    partner = device(z, y, 1 - c)
    y_of = [lax.rem(y + j, ny) for j in range(ny)]
    z_of = [lax.rem(z + j, nz) for j in range(nz)]
    y_back = [lax.rem(y + ny - j, ny) for j in range(ny)]
    z_back = [lax.rem(z + nz - j, nz) for j in range(nz)]

    def column(t):
        k = t // (2 * tiles)
        h = lax.rem(t // tiles, 2)
        i = lax.rem(t, tiles)
        core = jnp.where(h == 0, 1 - c, c)
        owner = (lax.rem(i, nz) * ny + i // nz) * CORES + core
        return pl.multiple_of(owner * owned + k * width, 128)

    def fetch(t):
        slot = lax.rem(t, BUFFERS)
        return pltpu.make_async_copy(
            w_ref.at[:, pl.ds(column(t), width)], wbuf.at[slot], wsem.at[slot]
        )

    for t in range(min(BUFFERS - 1, total_tiles)):
        fetch(jnp.int32(t)).start()

    barrier = pltpu.get_barrier_semaphore()
    peers = [partner]
    peers += [device(z, y_of[j], c) for j in range(1, ny)]
    peers += [device(z_of[j], y, c) for j in range(1, nz)]
    for peer in peers:
        pl.semaphore_signal(barrier, inc=1, device_id=peer, device_id_type=MESH)
    pl.semaphore_wait(barrier, len(peers))

    def remote(src, dst, send, recv, peer):
        return pltpu.make_async_remote_copy(
            src_ref=src, dst_ref=dst, send_sem=send, recv_sem=recv,
            device_id=peer, device_id_type=MESH,
        )

    def core_copy(k):
        return remote(cs.at[k], cr.at[k], cs_sem.at[k], cr_sem.at[k], partner)

    def y_copy(k, j):
        return remote(ys.at[k, j - 1], yr.at[k, j - 1], ys_sem.at[k, j - 1],
                      yr_sem.at[k, j - 1], device(z, y_of[j], c))

    def z_copy(k, j):
        return remote(zs.at[k, j - 1], zr.at[k, j - 1], zs_sem.at[k, j - 1],
                      zr_sem.at[k, j - 1], device(z_of[j], y, c))

    def block_of(k, yi, zi):
        owner = (zi * ny + yi) * CORES + c
        return out_ref.at[:, pl.ds(pl.multiple_of(owner * owned + k * width, 128), width)]

    def local_copy(k):
        return pltpu.make_async_copy(fin.at[k], block_of(k, y, z), loc_sem.at[k])

    def gather_z(k, j):
        return remote(fin.at[k], block_of(k, y, z), gzs_sem.at[k, j - 1],
                      gzr_sem.at[k, j - 1], device(z_of[j], y, c))

    def gather_y(k, j, b):
        block = block_of(k, y, z_back[b])
        return remote(block, block, gys_sem.at[k, j - 1, b], gyr_sem.at[k, j - 1, b],
                      device(z, y_of[j], c))

    def gather_core(k, a, b):
        block = block_of(k, y_back[a], z_back[b])
        return remote(block, block, gcs_sem.at[k, a, b], gcr_sem.at[k, a, b], partner)

    def multiply(k, h):
        first = (k * 2 + h) * tiles

        @pl.loop(0, tiles)
        def _(i):
            t = first + i

            @pl.when(t + BUFFERS - 1 < total_tiles)
            def _():
                fetch(t + BUFFERS - 1).start()

            fetch(t).wait()
            value = jnp.dot(
                hid_ref[...], wbuf[lax.rem(t, BUFFERS)], preferred_element_type=jnp.float32
            )
            value = value * hs_ref[...] * ws_ref[:, pl.ds(column(t), width)]
            if h == 0:
                cs[k, i // nz, lax.rem(i, nz)] = value.astype(cs.dtype)
            else:
                mine[k, i // nz, lax.rem(i, nz)] = value

    def send_y(k):
        core_copy(k).wait_recv()
        for j in range(1, ny):
            @pl.loop(0, nz)
            def _(b):
                ys[k, j - 1, b] = (
                    mine[k, y_of[j], b] + cr[k, y_of[j], b].astype(jnp.float32)
                ).astype(ys.dtype)

            y_copy(k, j).start()

        @pl.loop(0, nz)
        def _(b):
            mine[k, y, b] += cr[k, y, b].astype(jnp.float32)

    def send_z(k):
        for j in range(1, ny):
            y_copy(k, j).wait_recv()

        def total(b):
            value = mine[k, y, b]
            for j in range(1, ny):
                value += yr[k, j - 1, b].astype(jnp.float32)
            return value

        for j in range(1, nz):
            zs[k, j - 1] = total(z_of[j]).astype(zs.dtype)
            z_copy(k, j).start()
        mine[k, y, z] = total(z)

    def finish(k):
        value = mine[k, y, z] + res_ref[:, k * width:(k + 1) * width].astype(jnp.float32)
        for j in range(1, nz):
            z_copy(k, j).wait_recv()
            value += zr[k, j - 1].astype(jnp.float32)
        for b in range(width // BLOCK):
            part = value[:, b * BLOCK:(b + 1) * BLOCK]
            scale = jnp.max(jnp.abs(part), axis=1, keepdims=True) + 1e-6
            code = (part / scale).astype(jnp.bfloat16)
            fin[k, :, b * BLOCK:(b + 1) * BLOCK] = (
                code.astype(jnp.float32) * scale
            ).astype(fin.dtype)
        for j in range(1, nz):
            gather_z(k, j).start()
        local_copy(k).start()

    def pass_y(k):
        for b in range(nz):
            if b == 0:
                local_copy(k).wait()
            else:
                gather_z(k, b).wait_recv()
            for j in range(1, ny):
                gather_y(k, j, b).start()
            gather_core(k, 0, b).start()

    def pass_core(k):
        for b in range(nz):
            for j in range(1, ny):
                gather_y(k, j, b).wait_recv()
                gather_core(k, j, b).start()

    def drain(k):
        for a in range(ny):
            for b in range(nz):
                gather_core(k, a, b).wait()
        core_copy(k).wait_send()
        for j in range(1, ny):
            y_copy(k, j).wait_send()
            for b in range(nz):
                gather_y(k, j, b).wait_send()
        for j in range(1, nz):
            z_copy(k, j).wait_send()
            gather_z(k, j).wait_send()

    stages = ((send_y, 1), (send_z, 3), (finish, 5), (pass_y, 7), (pass_core, 9))
    for u in range(2 * chunks + 8):
        k, h = u // 2, u % 2
        if k < chunks:
            multiply(k, h)
            if h == 0:
                core_copy(k).start()
        for stage, lag in reversed(stages):
            if (u - lag) % 2 == 0 and 0 <= (u - lag) // 2 < chunks:
                stage((u - lag) // 2)
    for k in range(chunks):
        drain(k)


def shards(hidden_codes, hidden_scale, down_codes, weight_scale, residual):
    devices = lax.axis_size("tp")
    nz, ny = grid_of(devices)
    rows, depth = hidden_codes.shape
    model_width = down_codes.shape[1]
    owned = model_width // devices
    width = min(WIDTH, owned)
    chunks = owned // width
    bf16, f32 = jnp.bfloat16, jnp.float32
    vmem = pl.BlockSpec(memory_space=pltpu.VMEM)
    dma = pltpu.SemaphoreType.DMA
    tile = (rows, width)
    got = pl.pallas_call(
        functools.partial(kernel, nz, ny, width, chunks),
        out_shape=jax.ShapeDtypeStruct((rows, model_width), bf16),
        in_specs=[vmem, vmem, vmem, vmem, pl.BlockSpec(memory_space=pl.ANY)],
        out_specs=pl.BlockSpec(memory_space=pl.ANY),
        scratch_shapes=[
            pltpu.VMEM((BUFFERS, depth, width), bf16),
            pltpu.VMEM((chunks, ny, nz) + tile, f32),
            pltpu.VMEM((chunks, ny, nz) + tile, bf16),
            pltpu.VMEM((chunks, ny, nz) + tile, bf16),
            pltpu.VMEM((chunks, ny - 1, nz) + tile, bf16),
            pltpu.VMEM((chunks, ny - 1, nz) + tile, bf16),
            pltpu.VMEM((chunks, nz - 1) + tile, bf16),
            pltpu.VMEM((chunks, nz - 1) + tile, bf16),
            pltpu.VMEM((chunks,) + tile, bf16),
            dma((BUFFERS,)), dma((chunks,)), dma((chunks,)),
            dma((chunks, ny - 1)), dma((chunks, ny - 1)),
            dma((chunks, nz - 1)), dma((chunks, nz - 1)), dma((chunks,)),
            dma((chunks, nz - 1)), dma((chunks, nz - 1)),
            dma((chunks, ny - 1, nz)), dma((chunks, ny - 1, nz)),
            dma((chunks, ny, nz)), dma((chunks, ny, nz)),
        ],
        compiler_params=pltpu.CompilerParams(
            collective_id=0, has_side_effects=True, vmem_limit_bytes=48 * 1024 * 1024
        ),
        cost_estimate=pl.CostEstimate(
            flops=2 * rows * depth * model_width,
            bytes_accessed=2 * depth * model_width,
            transcendentals=0,
        ),
    )(hidden_codes, hidden_scale[:, None], weight_scale[None, :], residual, down_codes)
    return got


def solution(mesh):
    placed = (P("rep", "tp"), P("rep"), P("tp", None), P(), P("rep", "tp"))
    return jax.shard_map(
        shards, mesh=mesh, in_specs=placed, out_specs=P("rep", None), check_vma=False
    )
```

```python
import functools

import jax
import jax.numpy as jnp
from jax import lax
from jax.experimental import pallas as pl
from jax.experimental.pallas import tpu as pltpu
from jax.sharding import PartitionSpec as P

BLOCK = 128
CORES = 2
WIDTH = 256
BUFFERS = 8
MESH = pl.DeviceIdType.MESH


def grid_of(devices):
    chips = devices // CORES
    inner = 1
    while (2 * inner) ** 2 <= chips:
        inner *= 2
    return chips // inner, inner


def kernel(
    nz, ny, width, chunks,
    hid_ref, hs_ref, ws_ref, res_ref, w_ref, out_ref,
    wbuf, mine, cs, cr, ys, yr, zs, zr, fin,
    wsem, cs_sem, cr_sem, ys_sem, yr_sem, zs_sem, zr_sem, loc_sem,
    gzs_sem, gzr_sem, gys_sem, gyr_sem, gcs_sem, gcr_sem,
):
    me = lax.axis_index("tp")
    c = lax.rem(me, CORES)
    y = lax.rem(me // CORES, ny)
    z = me // (CORES * ny)
    owned = chunks * width
    tiles = ny * nz
    total_tiles = chunks * 2 * tiles

    def device(zi, yi, ci):
        return {"tp": (zi * ny + yi) * CORES + ci}

    partner = device(z, y, 1 - c)
    y_of = [lax.rem(y + j, ny) for j in range(ny)]
    z_of = [lax.rem(z + j, nz) for j in range(nz)]
    y_back = [lax.rem(y + ny - j, ny) for j in range(ny)]
    z_back = [lax.rem(z + nz - j, nz) for j in range(nz)]

    def column(t):
        k = t // (2 * tiles)
        h = lax.rem(t // tiles, 2)
        i = lax.rem(t, tiles)
        core = jnp.where(h == 0, 1 - c, c)
        owner = (lax.rem(i, nz) * ny + i // nz) * CORES + core
        return pl.multiple_of(owner * owned + k * width, 128)

    def fetch(t):
        slot = lax.rem(t, BUFFERS)
        return pltpu.make_async_copy(
            w_ref.at[:, pl.ds(column(t), width)], wbuf.at[slot], wsem.at[slot]
        )

    for t in range(min(BUFFERS - 1, total_tiles)):
        fetch(jnp.int32(t)).start()

    barrier = pltpu.get_barrier_semaphore()
    peers = [partner]
    peers += [device(z, y_of[j], c) for j in range(1, ny)]
    peers += [device(z_of[j], y, c) for j in range(1, nz)]
    for peer in peers:
        pl.semaphore_signal(barrier, inc=1, device_id=peer, device_id_type=MESH)
    pl.semaphore_wait(barrier, len(peers))

    def remote(src, dst, send, recv, peer):
        return pltpu.make_async_remote_copy(
            src_ref=src, dst_ref=dst, send_sem=send, recv_sem=recv,
            device_id=peer, device_id_type=MESH,
        )

    def core_copy(k):
        return remote(cs.at[k], cr.at[k], cs_sem.at[k], cr_sem.at[k], partner)

    def y_copy(k, j):
        return remote(ys.at[k, j - 1], yr.at[k, j - 1], ys_sem.at[k, j - 1],
                      yr_sem.at[k, j - 1], device(z, y_of[j], c))

    def z_copy(k, j):
        return remote(zs.at[k, j - 1], zr.at[k, j - 1], zs_sem.at[k, j - 1],
                      zr_sem.at[k, j - 1], device(z_of[j], y, c))

    def block_of(k, yi, zi):
        owner = (zi * ny + yi) * CORES + c
        return out_ref.at[:, pl.ds(pl.multiple_of(owner * owned + k * width, 128), width)]

    def local_copy(k):
        return pltpu.make_async_copy(fin.at[k], block_of(k, y, z), loc_sem.at[k])

    def gather_z(k, j):
        return remote(fin.at[k], block_of(k, y, z), gzs_sem.at[k, j - 1],
                      gzr_sem.at[k, j - 1], device(z_of[j], y, c))

    def gather_y(k, j, b):
        block = block_of(k, y, z_back[b])
        return remote(block, block, gys_sem.at[k, j - 1, b], gyr_sem.at[k, j - 1, b],
                      device(z, y_of[j], c))

    def gather_core(k, a, b):
        block = block_of(k, y_back[a], z_back[b])
        return remote(block, block, gcs_sem.at[k, a, b], gcr_sem.at[k, a, b], partner)

    def multiply(k, h):
        first = (k * 2 + h) * tiles

        @pl.loop(0, tiles)
        def _(i):
            t = first + i

            @pl.when(t + BUFFERS - 1 < total_tiles)
            def _():
                fetch(t + BUFFERS - 1).start()

            fetch(t).wait()
            value = jnp.dot(
                hid_ref[...], wbuf[lax.rem(t, BUFFERS)], preferred_element_type=jnp.float32
            )
            value = value * hs_ref[...] * ws_ref[:, pl.ds(column(t), width)]
            if h == 0:
                cs[k, i // nz, lax.rem(i, nz)] = value.astype(cs.dtype)
            else:
                mine[k, i // nz, lax.rem(i, nz)] = value

    def send_y(k):
        core_copy(k).wait_recv()
        for j in range(1, ny):
            @pl.loop(0, nz)
            def _(b):
                ys[k, j - 1, b] = (
                    mine[k, y_of[j], b] + cr[k, y_of[j], b].astype(jnp.float32)
                ).astype(ys.dtype)

            y_copy(k, j).start()

        @pl.loop(0, nz)
        def _(b):
            mine[k, y, b] += cr[k, y, b].astype(jnp.float32)

    def send_z(k):
        for j in range(1, ny):
            y_copy(k, j).wait_recv()

        def total(b):
            value = mine[k, y, b]
            for j in range(1, ny):
                value += yr[k, j - 1, b].astype(jnp.float32)
            return value

        for j in range(1, nz):
            zs[k, j - 1] = total(z_of[j]).astype(zs.dtype)
            z_copy(k, j).start()
        mine[k, y, z] = total(z)

    def finish(k):
        value = mine[k, y, z] + res_ref[:, k * width:(k + 1) * width].astype(jnp.float32)
        for j in range(1, nz):
            z_copy(k, j).wait_recv()
            value += zr[k, j - 1].astype(jnp.float32)
        for b in range(width // BLOCK):
            part = value[:, b * BLOCK:(b + 1) * BLOCK]
            scale = jnp.max(jnp.abs(part), axis=1, keepdims=True) + 1e-6
            code = (part / scale).astype(jnp.bfloat16)
            fin[k, :, b * BLOCK:(b + 1) * BLOCK] = (
                code.astype(jnp.float32) * scale
            ).astype(fin.dtype)
        for j in range(1, nz):
            gather_z(k, j).start()
        local_copy(k).start()

    def pass_y(k):
        for b in range(nz):
            if b == 0:
                local_copy(k).wait()
            else:
                gather_z(k, b).wait_recv()
            for j in range(1, ny):
                gather_y(k, j, b).start()
            gather_core(k, 0, b).start()

    def pass_core(k):
        for b in range(nz):
            for j in range(1, ny):
                gather_y(k, j, b).wait_recv()
                gather_core(k, j, b).start()

    def drain(k):
        for a in range(ny):
            for b in range(nz):
                gather_core(k, a, b).wait()
        core_copy(k).wait_send()
        for j in range(1, ny):
            y_copy(k, j).wait_send()
            for b in range(nz):
                gather_y(k, j, b).wait_send()
        for j in range(1, nz):
            z_copy(k, j).wait_send()
            gather_z(k, j).wait_send()

    stages = ((send_y, 1), (send_z, 3), (finish, 5), (pass_y, 7), (pass_core, 9))
    for u in range(2 * chunks + 8):
        k, h = u // 2, u % 2
        if k < chunks:
            multiply(k, h)
            if h == 0:
                core_copy(k).start()
        for stage, lag in stages:
            if (u - lag) % 2 == 0 and 0 <= (u - lag) // 2 < chunks:
                stage((u - lag) // 2)
    for k in range(chunks):
        drain(k)


def shards(hidden_codes, hidden_scale, down_codes, weight_scale, residual):
    devices = lax.axis_size("tp")
    nz, ny = grid_of(devices)
    rows, depth = hidden_codes.shape
    model_width = down_codes.shape[1]
    owned = model_width // devices
    width = min(WIDTH, owned)
    chunks = owned // width
    bf16, f32 = jnp.bfloat16, jnp.float32
    vmem = pl.BlockSpec(memory_space=pltpu.VMEM)
    dma = pltpu.SemaphoreType.DMA
    tile = (rows, width)
    got = pl.pallas_call(
        functools.partial(kernel, nz, ny, width, chunks),
        out_shape=jax.ShapeDtypeStruct((rows, model_width), bf16),
        in_specs=[vmem, vmem, vmem, vmem, pl.BlockSpec(memory_space=pl.ANY)],
        out_specs=vmem,
        scratch_shapes=[
            pltpu.VMEM((BUFFERS, depth, width), bf16),
            pltpu.VMEM((chunks, ny, nz) + tile, f32),
            pltpu.VMEM((chunks, ny, nz) + tile, bf16),
            pltpu.VMEM((chunks, ny, nz) + tile, bf16),
            pltpu.VMEM((chunks, ny - 1, nz) + tile, bf16),
            pltpu.VMEM((chunks, ny - 1, nz) + tile, bf16),
            pltpu.VMEM((chunks, nz - 1) + tile, bf16),
            pltpu.VMEM((chunks, nz - 1) + tile, bf16),
            pltpu.VMEM((chunks,) + tile, bf16),
            dma((BUFFERS,)), dma((chunks,)), dma((chunks,)),
            dma((chunks, ny - 1)), dma((chunks, ny - 1)),
            dma((chunks, nz - 1)), dma((chunks, nz - 1)), dma((chunks,)),
            dma((chunks, nz - 1)), dma((chunks, nz - 1)),
            dma((chunks, ny - 1, nz)), dma((chunks, ny - 1, nz)),
            dma((chunks, ny, nz)), dma((chunks, ny, nz)),
        ],
        compiler_params=pltpu.CompilerParams(
            collective_id=0, has_side_effects=True, vmem_limit_bytes=48 * 1024 * 1024
        ),
        cost_estimate=pl.CostEstimate(
            flops=2 * rows * depth * model_width,
            bytes_accessed=2 * depth * model_width,
            transcendentals=0,
        ),
    )(hidden_codes, hidden_scale[:, None], weight_scale[None, :], residual, down_codes)
    return got


def solution(mesh):
    placed = (P("rep", "tp"), P("rep"), P("tp", None), P(), P("rep", "tp"))
    return jax.shard_map(
        shards, mesh=mesh, in_specs=placed, out_specs=P("rep", None), check_vma=False
    )
```
